32 devices in a mesh: pair: 8 (over z, y), sec: 4 (over x, core).
Axes of the slice: x: 2, y: 2, z: 4, core: 2. Of those that a mesh axis runs over, the one named last changes fastest.
Arguments:
- psi: bfloat16 [32, 768, 384], P('sec'), may hold values from -6 to 6
- sec_rows: int32 [32], replicated, may hold values from 128 to 768, as said below
- match: int32 [32], replicated, may hold values from 0 to 31, each once
- normal_ops: bfloat16 [8, 32, 768, 768], P('pair', 'sec'), may hold values from -0.078125 to 0.078125
- comp_ops: bfloat16 [8, 32, 384, 384], P('pair', 'sec'), may hold values from -0.3125 to 0.3125
Outputs:
- sigma: bfloat16 [32, 768, 384], P('sec', 'pair')
The draws below stay inside these ranges and needn't reach their ends.
Inputs may be any that keep to these rules, and one draw needn't show every extreme that they name: `sec_rows`: every entry is a multiple of 128; some entry equals 768 in every draw.
All inputs are finite; a program needn't handle non-finite values.
Results may differ from the reference program's by a relative error of at most 0.0049.
Values may be sent and summed in bfloat16 or wider, within the bound.
A program may use at most 128 MiB of HBM per device.

```python
import jax
import jax.numpy as jnp
from jax import lax

MB = 768
NB = 384
ROW_UNIT = 128
SECTORS = 32
PAIRS = 8


def draw_sec_rows(key, part):
    units = MB // ROW_UNIT
    first_key, second_key = jax.random.split(key)
    counts = jax.random.randint(first_key, (SECTORS,), 1, units + 1) * ROW_UNIT
    where_full = jax.random.randint(second_key, (), 0, SECTORS)
    return jnp.where(jnp.arange(SECTORS) == where_full, MB, counts).astype(jnp.int32)


def steps_of(rng, shape, cuts, smallest, top_value):
    def one(position, blocks):
        draws = jax.random.uniform(jax.random.fold_in(jax.random.fold_in(rng, 6), position), (blocks,), jnp.float32, smallest / len(cuts), top_value / len(cuts))
        return jnp.repeat(jnp.exp(draws), shape[position] // blocks).reshape((-1,) + (1,) * (len(shape) - position - 1))

    gain = one(*cuts[0])
    for cut in cuts[1:]:
        gain = gain * one(*cut)
    return gain


def normal_values(rng, extent, scale, reach, cuts=(), kind=jnp.bfloat16):
    level = steps_of(rng, extent, cuts, -0.22, 0.18) if cuts else 1.0
    entries = jax.random.normal(rng, extent, jnp.float32) * scale * level
    return jnp.minimum(jnp.maximum(entries, -reach), reach).astype(kind)


def setup_inputs(seed: int = 0) -> dict:
    keys = jax.random.split(jax.random.key(seed), 6)
    return {
        "psi": normal_values(keys[0], (SECTORS, MB, NB), 1.0, 6.0, ((0, 4),)),
        "sec_rows": draw_sec_rows(jax.random.fold_in(keys[5], 71), 0),
        "match": jax.random.permutation(keys[2], SECTORS).astype(jnp.int32),
        "normal_ops": normal_values(keys[3], (PAIRS, SECTORS, MB, MB), (MB * PAIRS) ** -0.5, 0.078125, ((0, 8), (1, 4))),
        "comp_ops": normal_values(keys[4], (PAIRS, SECTORS, NB, NB), NB ** -0.5, 0.3125, ((0, 8), (1, 4))),
    }


def reference(psi, sec_rows, match, normal_ops, comp_ops):
    line = jnp.arange(MB, dtype=jnp.int32)
    keep = line[None, :] < sec_rows[:, None]
    kept = jnp.where(keep[:, :, None], psi, jnp.zeros_like(psi))
    kept_wide = kept.astype(jnp.float32)

    def one_pair(total, index):
        left_op = normal_ops[index].astype(jnp.float32)
        right_op = comp_ops[PAIRS - 1 - index].astype(jnp.float32)
        half = jnp.einsum('sab,sbc->sac', left_op, kept_wide).astype(jnp.bfloat16)
        term = jnp.einsum('sac,sdc->sad', half.astype(jnp.float32), right_op)
        return total + term, None

    start = jnp.zeros((SECTORS, MB, NB), jnp.float32)
    images, _ = lax.scan(one_pair, start, jnp.arange(PAIRS, dtype=jnp.int32))
    placed = jnp.zeros((SECTORS, MB, NB), jnp.float32).at[match].set(images)
    out_keep = line[None, :] < sec_rows[:, None]
    placed = jnp.where(out_keep[:, :, None], placed, jnp.zeros_like(placed))
    return placed.astype(jnp.bfloat16)
```

```python
import functools

import jax
import jax.numpy as jnp
from jax import lax
from jax.experimental import pallas as pl
from jax.experimental.pallas import tpu as pltpu
from jax.sharding import PartitionSpec as P

WINDOW = 2
MESH = pl.DeviceIdType.MESH


def pick_sources(gathered, match, targets):
    total = match.shape[0]
    hits = match[None, :] == targets[:, None]
    source = jnp.sum(jnp.where(hits, jnp.arange(total, dtype=jnp.int32)[None, :], 0), axis=1)
    return gathered[source]


def shards(psi, sec_rows, match, normal_ops, comp_ops):
    sec_dev = psi.shape[0]
    block_rows = psi.shape[1]
    first = lax.axis_index("sec") * sec_dev
    targets = first + jnp.arange(sec_dev, dtype=jnp.int32)
    rows_here = lax.dynamic_slice_in_dim(sec_rows, first, sec_dev)
    line = jnp.arange(block_rows, dtype=jnp.int32)
    kept = jnp.where((line[None, :] < rows_here[:, None])[:, :, None], psi, jnp.zeros_like(psi))
    spread = lax.all_to_all(comp_ops, "pair", split_axis=2, concat_axis=0, tiled=True)
    mirrored = lax.all_to_all(spread[::-1], "pair", split_axis=0, concat_axis=2, tiled=True)
    half = jnp.einsum(
        "psab,sbc->psac", normal_ops, kept, preferred_element_type=jnp.float32
    ).astype(jnp.bfloat16)
    terms = jnp.einsum("psac,psdc->sad", half, mirrored, preferred_element_type=jnp.float32)
    share = block_rows // lax.axis_size("pair")
    row_start = lax.axis_index("pair") * share
    partial_rows = lax.psum_scatter(terms, "pair", scatter_dimension=1, tiled=True).astype(
        jnp.bfloat16
    )
    gathered = lax.all_gather(partial_rows, "sec", axis=0, tiled=True)
    summed = pick_sources(gathered, match, targets)
    target_rows = lax.dynamic_slice_in_dim(sec_rows, first, sec_dev)
    my_lines = row_start + jnp.arange(share, dtype=jnp.int32)
    out_keep = my_lines[None, :] < target_rows[:, None]
    return jnp.where(out_keep[:, :, None], summed, jnp.zeros_like(summed))


def kernel(
    secs, rows_ref, psi_ref, norm_ref, comp_ref, out_ref,
    psi_v, norm_v, half_v, comp_v, acc, s1, r1, s2, r2, s3, r3, s4,
    psi_sem, norm_sem, csend, crecv, send1, recv1, send2, recv2, send3, recv3,
    send4, recv4, local_sem,
):
    n = psi_ref.shape[0]
    mb, nb = psi_ref.shape[1:]
    share = mb // 8
    bf16 = jnp.bfloat16
    pair = lax.axis_index("pair")
    sec = lax.axis_index("sec")
    y = pair % 2
    z = pair // 2
    zl = z % 2
    zh = z // 2
    mirror = (7 - pair, sec)
    y_peer = (z * 2 + 1 - y, sec)
    zl_peer = ((zh * 2 + 1 - zl) * 2 + y, sec)
    zh_peer = (((1 - zh) * 2 + zl) * 2 + y, sec)
    sec_peers = [(pair, (sec + k) % secs) for k in range(1, secs)]

    def load(s):
        return (
            pltpu.make_async_copy(psi_ref.at[s], psi_v.at[s], psi_sem.at[s]),
            pltpu.make_async_copy(norm_ref.at[0, s], norm_v.at[s], norm_sem.at[s]),
        )

    def remote(src, dst, send, recv, where):
        return pltpu.make_async_remote_copy(
            src_ref=src, dst_ref=dst, send_sem=send, recv_sem=recv,
            device_id=where, device_id_type=MESH,
        )

    def comp_copy(s):
        return remote(comp_ref.at[0, s], comp_v.at[s], csend.at[s], crecv.at[s], mirror)

    def copy1(s):
        return remote(s1.at[s], r1.at[s], send1.at[s], recv1.at[s], y_peer)

    def copy2(s):
        return remote(s2.at[s], r2.at[s], send2.at[s], recv2.at[s], zl_peer)

    def copy3(s):
        return remote(s3.at[s], r3.at[s], send3.at[s], recv3.at[s], zh_peer)

    def copy4(s, k):
        return remote(
            s4.at[s], out_ref.at[sec * n + s], send4.at[k, s], recv4.at[k, s], sec_peers[k]
        )

    def keep4(s):
        return pltpu.make_async_copy(s4.at[s], out_ref.at[sec * n + s], local_sem.at[s])

    barrier = pltpu.get_barrier_semaphore()
    peers = [mirror, y_peer, zl_peer, zh_peer] + sec_peers
    for peer in peers:
        pl.semaphore_signal(barrier, inc=1, device_id=peer, device_id_type=MESH)
    for s in range(n):
        for c in load(s):
            c.start()
    pl.semaphore_wait(barrier, len(peers))
    for s in range(WINDOW):
        comp_copy(s).start()

    @pl.loop(0, n)
    def _(s):
        for c in load(s):
            c.wait()
        line = lax.broadcasted_iota(jnp.int32, (mb, nb), 0)
        value = psi_v[s].astype(jnp.float32)
        kept = jnp.where(line < rows_ref[sec * n + s], value, 0.0).astype(bf16)
        got = jnp.dot(norm_v[s], kept, preferred_element_type=jnp.float32).astype(bf16)
        for b in range(8):
            half_v[s, b % 2, b // 2] = got[b * share : (b + 1) * share]

    def image(s, which):
        rows = half_v[s, which].reshape(mb // 2, nb)
        return lax.dot_general(
            rows, comp_v[s], (((1,), (1,)), ((), ())), preferred_element_type=jnp.float32
        )

    @pl.loop(0, n + 3)
    def _(step):
        @pl.when(step >= 3)
        def _():
            s = step - 3
            copy3(s).wait()
            s4[s] = (acc[s, zh, zl] + r3[s].astype(jnp.float32)).astype(bf16)
            keep4(s).start()
            for k in range(secs - 1):
                copy4(s, k).start()

        @pl.when((step >= 2) & (step < n + 2))
        def _():
            s = step - 2
            copy2(s).wait()
            s3[s] = (acc[s, 1 - zh, zl] + r2[s, 1 - zh].astype(jnp.float32)).astype(bf16)
            copy3(s).start()
            acc[s, zh, zl] = acc[s, zh, zl] + r2[s, zh].astype(jnp.float32)

        @pl.when((step >= 1) & (step < n + 1))
        def _():
            s = step - 1
            copy1(s).wait()
            for h in range(2):
                s2[s, h] = (acc[s, h, 1 - zl] + r1[s, h, 1 - zl].astype(jnp.float32)).astype(bf16)
            copy2(s).start()
            for h in range(2):
                acc[s, h, zl] = acc[s, h, zl] + r1[s, h, zl].astype(jnp.float32)

        @pl.when(step < n)
        def _():
            s = step
            comp_copy(s).wait()

            @pl.when(s + WINDOW < n)
            def _():
                comp_copy(s + WINDOW).start()

            s1[s] = image(s, 1 - y).astype(bf16).reshape(2, 2, share, nb)
            copy1(s).start()
            acc[s] = image(s, y).reshape(2, 2, share, nb)

    @pl.loop(0, n)
    def _(s):
        keep4(s).wait()
        for k in range(secs - 1):
            copy4(s, k).wait()


def place_kernel(source_ref, rows_ref, start_ref, in_ref, out_ref):
    t = pl.program_id(0)
    share, nb = out_ref.shape[1:]
    line = start_ref[0] + lax.broadcasted_iota(jnp.int32, (share, nb), 0)
    value = in_ref[0].astype(jnp.float32)
    out_ref[0] = jnp.where(line < rows_ref[t], value, 0.0).astype(out_ref.dtype)


def kernel_shards(secs, psi, sec_rows, match, normal_ops, comp_ops):
    n, mb, nb = psi.shape
    total = match.shape[0]
    share = mb // 8
    bf16 = jnp.bfloat16
    vmem = pltpu.VMEM
    dma = pltpu.SemaphoreType.DMA
    gathered = pl.pallas_call(
        functools.partial(kernel, secs),
        out_shape=jax.ShapeDtypeStruct((total, share, nb), bf16),
        in_specs=[pl.BlockSpec(memory_space=pltpu.SMEM)] + [pl.BlockSpec(memory_space=pl.ANY)] * 3,
        out_specs=pl.BlockSpec(memory_space=pl.ANY),
        scratch_shapes=[
            vmem((n, mb, nb), bf16),
            vmem((n, mb, mb), bf16),
            vmem((n, 2, 4, share, nb), bf16),
            vmem((n, nb, nb), bf16),
            vmem((n, 2, 2, share, nb), jnp.float32),
            vmem((n, 2, 2, share, nb), bf16),
            vmem((n, 2, 2, share, nb), bf16),
            vmem((n, 2, share, nb), bf16),
            vmem((n, 2, share, nb), bf16),
            vmem((n, share, nb), bf16),
            vmem((n, share, nb), bf16),
            vmem((n, share, nb), bf16),
        ]
        + [dma((n,))] * 10
        + [dma((secs - 1, n))] * 2
        + [dma((n,))],
        compiler_params=pltpu.CompilerParams(
            collective_id=0, has_side_effects=True, vmem_limit_bytes=56 * 1024 * 1024
        ),
        cost_estimate=pl.CostEstimate(
            flops=2 * n * mb * nb * (mb + nb), bytes_accessed=20_000_000, transcendentals=0
        ),
    )(sec_rows, psi, normal_ops, comp_ops)

    first = lax.axis_index("sec") * n
    targets = first + jnp.arange(n, dtype=jnp.int32)
    hits = match[None, :] == targets[:, None]
    source = jnp.sum(jnp.where(hits, jnp.arange(total, dtype=jnp.int32)[None, :], 0), axis=1)
    target_rows = lax.dynamic_slice_in_dim(sec_rows, first, n)
    start = (lax.axis_index("pair") * share).astype(jnp.int32)[None]
    return pl.pallas_call(
        place_kernel,
        out_shape=jax.ShapeDtypeStruct((n, share, nb), bf16),
        grid_spec=pltpu.PrefetchScalarGridSpec(
            num_scalar_prefetch=3,
            grid=(n,),
            in_specs=[pl.BlockSpec((1, share, nb), lambda t, src, rows, st: (src[t], 0, 0))],
            out_specs=pl.BlockSpec((1, share, nb), lambda t, src, rows, st: (t, 0, 0)),
        ),
    )(source, target_rows, start, gathered)


def solution(mesh):
    in_specs = (
        P("sec", None, None),
        P(),
        P(),
        P("pair", "sec", None, None),
        P("pair", "sec", None, None),
    )
    out_specs = P("sec", "pair", None)
    body = shards
    if mesh.shape["pair"] == 8:
        body = functools.partial(kernel_shards, mesh.shape["sec"])
    return jax.shard_map(body, mesh=mesh, in_specs=in_specs, out_specs=out_specs, check_vma=False)
```

```python
import functools

import jax
import jax.numpy as jnp
from jax import lax
from jax.experimental import pallas as pl
from jax.experimental.pallas import tpu as pltpu
from jax.sharding import PartitionSpec as P

WINDOW = 4
LAGS = (3, 6, 9)
LANES = 128
MESH = pl.DeviceIdType.MESH


def pick_sources(gathered, match, targets):
    total = match.shape[0]
    hits = match[None, :] == targets[:, None]
    source = jnp.sum(jnp.where(hits, jnp.arange(total, dtype=jnp.int32)[None, :], 0), axis=1)
    return gathered[source]


def shards(psi, sec_rows, match, normal_ops, comp_ops):
    sec_dev = psi.shape[0]
    block_rows = psi.shape[1]
    first = lax.axis_index("sec") * sec_dev
    targets = first + jnp.arange(sec_dev, dtype=jnp.int32)
    rows_here = lax.dynamic_slice_in_dim(sec_rows, first, sec_dev)
    line = jnp.arange(block_rows, dtype=jnp.int32)
    kept = jnp.where((line[None, :] < rows_here[:, None])[:, :, None], psi, jnp.zeros_like(psi))
    spread = lax.all_to_all(comp_ops, "pair", split_axis=2, concat_axis=0, tiled=True)
    mirrored = lax.all_to_all(spread[::-1], "pair", split_axis=0, concat_axis=2, tiled=True)
    half = jnp.einsum(
        "psab,sbc->psac", normal_ops, kept, preferred_element_type=jnp.float32
    ).astype(jnp.bfloat16)
    terms = jnp.einsum("psac,psdc->sad", half, mirrored, preferred_element_type=jnp.float32)
    share = block_rows // lax.axis_size("pair")
    row_start = lax.axis_index("pair") * share
    partial_rows = lax.psum_scatter(terms, "pair", scatter_dimension=1, tiled=True).astype(
        jnp.bfloat16
    )
    gathered = lax.all_gather(partial_rows, "sec", axis=0, tiled=True)
    summed = pick_sources(gathered, match, targets)
    target_rows = lax.dynamic_slice_in_dim(sec_rows, first, sec_dev)
    my_lines = row_start + jnp.arange(share, dtype=jnp.int32)
    out_keep = my_lines[None, :] < target_rows[:, None]
    return jnp.where(out_keep[:, :, None], summed, jnp.zeros_like(summed))


def kernel(
    secs, rows_ref, psi_ref, norm_ref, comp_ref, out_ref,
    psi_v, norm_v, half_v, comp_v, acc, s1, r1, s2, r2, s3, r3, s4,
    psi_sem, norm_sem, csend, crecv, send1, recv1, send2, recv2, send3, recv3,
    send4, recv4, local_sem,
):
    n = psi_ref.shape[0]
    mb, nb = psi_ref.shape[1:]
    cuts = nb // LANES
    pieces = n * cuts
    share = mb // 8
    lag2, lag3, lag4 = LAGS
    bf16 = jnp.bfloat16
    f32 = jnp.float32
    pair = lax.axis_index("pair")
    sec = lax.axis_index("sec")
    y = pair % 2
    z = pair // 2
    zl = z % 2
    zh = z // 2
    mirror = (7 - pair, sec)
    y_peer = (z * 2 + 1 - y, sec)
    zl_peer = ((zh * 2 + 1 - zl) * 2 + y, sec)
    zh_peer = (((1 - zh) * 2 + zl) * 2 + y, sec)
    sec_peers = [(pair, (sec + k) % secs) for k in range(1, secs)]

    def load(s):
        return (
            pltpu.make_async_copy(psi_ref.at[s], psi_v.at[s], psi_sem.at[s]),
            pltpu.make_async_copy(norm_ref.at[0, s], norm_v.at[s], norm_sem.at[s]),
        )

    def remote(src, dst, send, recv, where):
        return pltpu.make_async_remote_copy(
            src_ref=src, dst_ref=dst, send_sem=send, recv_sem=recv,
            device_id=where, device_id_type=MESH,
        )

    def comp_copy(j):
        lines = pl.ds(pl.multiple_of((j % cuts) * LANES, LANES), LANES)
        return remote(
            comp_ref.at[0, j // cuts, lines], comp_v.at[j], csend.at[j], crecv.at[j], mirror
        )

    def copy1(j):
        return remote(s1.at[j], r1.at[j], send1.at[j], recv1.at[j], y_peer)

    def copy2(j):
        return remote(s2.at[j], r2.at[j], send2.at[j], recv2.at[j], zl_peer)

    def copy3(j):
        return remote(s3.at[j], r3.at[j], send3.at[j], recv3.at[j], zh_peer)

    def copy4(j, k):
        return remote(
            s4.at[j], out_ref.at[sec * pieces + j], send4.at[k, j], recv4.at[k, j], sec_peers[k]
        )

    def keep4(j):
        return pltpu.make_async_copy(s4.at[j], out_ref.at[sec * pieces + j], local_sem.at[j])

    barrier = pltpu.get_barrier_semaphore()
    peers = [mirror, y_peer, zl_peer, zh_peer] + sec_peers
    for peer in peers:
        pl.semaphore_signal(barrier, inc=1, device_id=peer, device_id_type=MESH)
    for s in range(n):
        for c in load(s):
            c.start()
    pl.semaphore_wait(barrier, len(peers))
    for j in range(WINDOW):
        comp_copy(j).start()

    def make_half(s):
        for c in load(s):
            c.wait()
        line = lax.broadcasted_iota(jnp.int32, (mb, nb), 0)
        kept = jnp.where(line < rows_ref[sec * n + s], psi_v[s].astype(f32), 0.0).astype(bf16)
        got = jnp.dot(norm_v[s], kept, preferred_element_type=f32).astype(bf16)
        for b in range(8):
            half_v[s, b % 2, b // 2] = got[b * share : (b + 1) * share]

    make_half(0)

    def image(j, which):
        rows = half_v[j // cuts, which].reshape(mb // 2, nb)
        got = lax.dot_general(
            rows, comp_v[j], (((1,), (1,)), ((), ())), preferred_element_type=f32
        )
        return got.reshape(2, 2, share, LANES)

    @pl.loop(0, pieces + lag4)
    def _(step):
        @pl.when(step >= lag4)
        def _():
            j = step - lag4
            copy3(j).wait()
            s4[j] = (acc[j, zh, zl] + r3[j].astype(f32)).astype(bf16)
            keep4(j).start()
            for k in range(secs - 1):
                copy4(j, k).start()

        @pl.when((step >= lag3) & (step < pieces + lag3))
        def _():
            j = step - lag3
            copy2(j).wait()
            s3[j] = (acc[j, 1 - zh, zl] + r2[j, 1 - zh].astype(f32)).astype(bf16)
            copy3(j).start()
            acc[j, zh, zl] = acc[j, zh, zl] + r2[j, zh].astype(f32)

        @pl.when((step >= lag2) & (step < pieces + lag2))
        def _():
            j = step - lag2
            copy1(j).wait()
            for h in range(2):
                s2[j, h] = (acc[j, h, 1 - zl] + r1[j, h, 1 - zl].astype(f32)).astype(bf16)
            copy2(j).start()
            for h in range(2):
                acc[j, h, zl] = acc[j, h, zl] + r1[j, h, zl].astype(f32)

        @pl.when(step < pieces)
        def _():
            j = step
            comp_copy(j).wait()

            @pl.when(j + WINDOW < pieces)
            def _():
                comp_copy(j + WINDOW).start()

            s1[j] = image(j, 1 - y).astype(bf16)
            copy1(j).start()
            acc[j] = image(j, y)

            @pl.when((j % cuts == 0) & (j + cuts < pieces))
            def _():
                make_half(j // cuts + 1)

    @pl.loop(0, pieces)
    def _(j):
        keep4(j).wait()
        for k in range(secs - 1):
            copy4(j, k).wait()


def place_kernel(rows_ref, match_ref, in_ref, out_ref, source):
    n, share, nb = out_ref.shape
    first = lax.axis_index("sec") * n
    start = lax.axis_index("pair") * share
    cuts = nb // LANES

    for i in range(match_ref.shape[0]):
        t = match_ref[i] - first

        @pl.when((t >= 0) & (t < n))
        def _():
            source[t] = i

    @pl.loop(0, n)
    def _(t):
        line = start + lax.broadcasted_iota(jnp.int32, (share, LANES), 0)
        keep = line < rows_ref[first + t]
        for c in range(cuts):
            value = in_ref[source[t] * cuts + c].astype(jnp.float32)
            value = jnp.where(keep, value, 0.0).astype(out_ref.dtype)
            out_ref[t, :, c * LANES : (c + 1) * LANES] = value


def kernel_shards(secs, psi, sec_rows, match, normal_ops, comp_ops):
    n, mb, nb = psi.shape
    share = mb // 8
    pieces = n * (nb // LANES)
    bf16 = jnp.bfloat16
    vmem = pltpu.VMEM
    dma = pltpu.SemaphoreType.DMA
    gathered = pl.pallas_call(
        functools.partial(kernel, secs),
        out_shape=jax.ShapeDtypeStruct((secs * pieces, share, LANES), bf16),
        in_specs=[pl.BlockSpec(memory_space=pltpu.SMEM)] + [pl.BlockSpec(memory_space=pl.ANY)] * 3,
        out_specs=pl.BlockSpec(memory_space=pl.ANY),
        scratch_shapes=[
            vmem((n, mb, nb), bf16),
            vmem((n, mb, mb), bf16),
            vmem((n, 2, 4, share, nb), bf16),
            vmem((pieces, LANES, nb), bf16),
            vmem((pieces, 2, 2, share, LANES), jnp.float32),
            vmem((pieces, 2, 2, share, LANES), bf16),
            vmem((pieces, 2, 2, share, LANES), bf16),
            vmem((pieces, 2, share, LANES), bf16),
            vmem((pieces, 2, share, LANES), bf16),
            vmem((pieces, share, LANES), bf16),
            vmem((pieces, share, LANES), bf16),
            vmem((pieces, share, LANES), bf16),
        ]
        + [dma((n,))] * 2
        + [dma((pieces,))] * 8
        + [dma((secs - 1, pieces))] * 2
        + [dma((pieces,))],
        compiler_params=pltpu.CompilerParams(
            collective_id=0, has_side_effects=True, vmem_limit_bytes=56 * 1024 * 1024
        ),
        cost_estimate=pl.CostEstimate(
            flops=2 * n * mb * nb * (mb + nb), bytes_accessed=20_000_000, transcendentals=0
        ),
    )(sec_rows, psi, normal_ops, comp_ops)
    return pl.pallas_call(
        place_kernel,
        out_shape=jax.ShapeDtypeStruct((n, share, nb), bf16),
        in_specs=[pl.BlockSpec(memory_space=pltpu.SMEM)] * 2
        + [pl.BlockSpec(memory_space=pltpu.VMEM)],
        out_specs=pl.BlockSpec(memory_space=pltpu.VMEM),
        scratch_shapes=[pltpu.SMEM((n,), jnp.int32)],
        compiler_params=pltpu.CompilerParams(vmem_limit_bytes=16 * 1024 * 1024),
    )(sec_rows, match, gathered)


def solution(mesh):
    in_specs = (
        P("sec", None, None),
        P(),
        P(),
        P("pair", "sec", None, None),
        P("pair", "sec", None, None),
    )
    out_specs = P("sec", "pair", None)
    body = shards
    if mesh.shape["pair"] == 8:
        body = functools.partial(kernel_shards, mesh.shape["sec"])
    return jax.shard_map(body, mesh=mesh, in_specs=in_specs, out_specs=out_specs, check_vma=False)
```

```python
import functools

import jax
import jax.numpy as jnp
from jax import lax
from jax.experimental import pallas as pl
from jax.experimental.pallas import tpu as pltpu
from jax.sharding import PartitionSpec as P

WINDOW = 4
LAGS = (4, 8, 12)
LANES = 128
MESH = pl.DeviceIdType.MESH


def pick_sources(gathered, match, targets):
    total = match.shape[0]
    hits = match[None, :] == targets[:, None]
    source = jnp.sum(jnp.where(hits, jnp.arange(total, dtype=jnp.int32)[None, :], 0), axis=1)
    return gathered[source]


def shards(psi, sec_rows, match, normal_ops, comp_ops):
    sec_dev = psi.shape[0]
    block_rows = psi.shape[1]
    first = lax.axis_index("sec") * sec_dev
    targets = first + jnp.arange(sec_dev, dtype=jnp.int32)
    rows_here = lax.dynamic_slice_in_dim(sec_rows, first, sec_dev)
    line = jnp.arange(block_rows, dtype=jnp.int32)
    kept = jnp.where((line[None, :] < rows_here[:, None])[:, :, None], psi, jnp.zeros_like(psi))
    spread = lax.all_to_all(comp_ops, "pair", split_axis=2, concat_axis=0, tiled=True)
    mirrored = lax.all_to_all(spread[::-1], "pair", split_axis=0, concat_axis=2, tiled=True)
    half = jnp.einsum(
        "psab,sbc->psac", normal_ops, kept, preferred_element_type=jnp.float32
    ).astype(jnp.bfloat16)
    terms = jnp.einsum("psac,psdc->sad", half, mirrored, preferred_element_type=jnp.float32)
    share = block_rows // lax.axis_size("pair")
    row_start = lax.axis_index("pair") * share
    partial_rows = lax.psum_scatter(terms, "pair", scatter_dimension=1, tiled=True).astype(
        jnp.bfloat16
    )
    gathered = lax.all_gather(partial_rows, "sec", axis=0, tiled=True)
    summed = pick_sources(gathered, match, targets)
    target_rows = lax.dynamic_slice_in_dim(sec_rows, first, sec_dev)
    my_lines = row_start + jnp.arange(share, dtype=jnp.int32)
    out_keep = my_lines[None, :] < target_rows[:, None]
    return jnp.where(out_keep[:, :, None], summed, jnp.zeros_like(summed))


def kernel(
    secs, rows_ref, psi_ref, norm_ref, comp_ref, out_ref,
    psi_v, norm_v, half_v, comp_v, acc, s1, r1, s2, r2, s3, r3, s4,
    psi_sem, norm_sem, csend, crecv, send1, recv1, send2, recv2, send3, recv3,
    send4, recv4, local_sem,
):
    n = psi_ref.shape[0]
    mb, nb = psi_ref.shape[1:]
    cuts = nb // LANES
    pieces = n * cuts
    share = mb // 8
    lag2, lag3, lag4 = LAGS
    bf16 = jnp.bfloat16
    f32 = jnp.float32
    pair = lax.axis_index("pair")
    sec = lax.axis_index("sec")
    y = pair % 2
    z = pair // 2
    zl = z % 2
    zh = z // 2
    mirror = (7 - pair, sec)
    y_peer = (z * 2 + 1 - y, sec)
    zl_peer = ((zh * 2 + 1 - zl) * 2 + y, sec)
    zh_peer = (((1 - zh) * 2 + zl) * 2 + y, sec)
    sec_peers = [(pair, (sec + k) % secs) for k in range(1, secs)]

    def load(s):
        return (
            pltpu.make_async_copy(psi_ref.at[s], psi_v.at[s], psi_sem.at[s]),
            pltpu.make_async_copy(norm_ref.at[0, s], norm_v.at[s], norm_sem.at[s]),
        )

    def remote(src, dst, send, recv, where):
        return pltpu.make_async_remote_copy(
            src_ref=src, dst_ref=dst, send_sem=send, recv_sem=recv,
            device_id=where, device_id_type=MESH,
        )

    def comp_copy(j):
        lines = pl.ds(pl.multiple_of((j % cuts) * LANES, LANES), LANES)
        return remote(
            comp_ref.at[0, j // cuts, lines], comp_v.at[j], csend.at[j], crecv.at[j], mirror
        )

    def copy1(j):
        return remote(s1.at[j], r1.at[j], send1.at[j], recv1.at[j], y_peer)

    def copy2(j):
        return remote(s2.at[j], r2.at[j], send2.at[j], recv2.at[j], zl_peer)

    def copy3(j):
        return remote(s3.at[j], r3.at[j], send3.at[j], recv3.at[j], zh_peer)

    def copy4(j, k):
        return remote(
            s4.at[j], out_ref.at[sec * pieces + j], send4.at[k, j], recv4.at[k, j], sec_peers[k]
        )

    def keep4(j):
        return pltpu.make_async_copy(s4.at[j], out_ref.at[sec * pieces + j], local_sem.at[j])

    barrier = pltpu.get_barrier_semaphore()
    peers = [mirror, y_peer, zl_peer, zh_peer] + sec_peers
    for peer in peers:
        pl.semaphore_signal(barrier, inc=1, device_id=peer, device_id_type=MESH)
    for s in range(n):
        for c in load(s):
            c.start()
    pl.semaphore_wait(barrier, len(peers))
    for j in range(WINDOW):
        comp_copy(j).start()

    def make_half(s):
        for c in load(s):
            c.wait()
        line = lax.broadcasted_iota(jnp.int32, (mb, nb), 0)
        kept = jnp.where(line < rows_ref[sec * n + s], psi_v[s].astype(f32), 0.0).astype(bf16)
        got = jnp.dot(norm_v[s], kept, preferred_element_type=f32).astype(bf16)
        for b in range(8):
            half_v[s, b % 2, b // 2] = got[b * share : (b + 1) * share]

    make_half(0)

    def image(j, which):
        rows = half_v[j // cuts, which].reshape(mb // 2, nb)
        got = lax.dot_general(
            rows, comp_v[j], (((1,), (1,)), ((), ())), preferred_element_type=f32
        )
        return got.reshape(2, 2, share, LANES)

    @pl.loop(0, pieces + lag4)
    def _(step):
        @pl.when(step < pieces)
        def _():
            j = step
            comp_copy(j).wait()

            @pl.when(j + WINDOW < pieces)
            def _():
                comp_copy(j + WINDOW).start()

            s1[j] = image(j, 1 - y).astype(bf16)
            copy1(j).start()
            acc[j] = image(j, y)

            @pl.when((j % cuts == 0) & (j + cuts < pieces))
            def _():
                make_half(j // cuts + 1)

        @pl.when(step >= lag4)
        def _():
            j = step - lag4
            copy3(j).wait()
            s4[j] = (acc[j, zh, zl] + r3[j].astype(f32)).astype(bf16)
            keep4(j).start()
            for k in range(secs - 1):
                copy4(j, k).start()

        @pl.when((step >= lag3) & (step < pieces + lag3))
        def _():
            j = step - lag3
            copy2(j).wait()
            s3[j] = (acc[j, 1 - zh, zl] + r2[j, 1 - zh].astype(f32)).astype(bf16)
            copy3(j).start()
            acc[j, zh, zl] = acc[j, zh, zl] + r2[j, zh].astype(f32)

        @pl.when((step >= lag2) & (step < pieces + lag2))
        def _():
            j = step - lag2
            copy1(j).wait()
            for h in range(2):
                s2[j, h] = (acc[j, h, 1 - zl] + r1[j, h, 1 - zl].astype(f32)).astype(bf16)
            copy2(j).start()
            for h in range(2):
                acc[j, h, zl] = acc[j, h, zl] + r1[j, h, zl].astype(f32)

    @pl.loop(0, pieces)
    def _(j):
        keep4(j).wait()
        for k in range(secs - 1):
            copy4(j, k).wait()


def place_kernel(rows_ref, match_ref, in_ref, out_ref, source):
    n, share, nb = out_ref.shape
    first = lax.axis_index("sec") * n
    start = lax.axis_index("pair") * share
    cuts = nb // LANES

    for i in range(match_ref.shape[0]):
        t = match_ref[i] - first

        @pl.when((t >= 0) & (t < n))
        def _():
            source[t] = i

    @pl.loop(0, n)
    def _(t):
        line = start + lax.broadcasted_iota(jnp.int32, (share, LANES), 0)
        keep = line < rows_ref[first + t]
        for c in range(cuts):
            value = in_ref[source[t] * cuts + c].astype(jnp.float32)
            value = jnp.where(keep, value, 0.0).astype(out_ref.dtype)
            out_ref[t, :, c * LANES : (c + 1) * LANES] = value


def kernel_shards(secs, psi, sec_rows, match, normal_ops, comp_ops):
    n, mb, nb = psi.shape
    share = mb // 8
    pieces = n * (nb // LANES)
    bf16 = jnp.bfloat16
    vmem = pltpu.VMEM
    dma = pltpu.SemaphoreType.DMA
    gathered = pl.pallas_call(
        functools.partial(kernel, secs),
        out_shape=jax.ShapeDtypeStruct((secs * pieces, share, LANES), bf16),
        in_specs=[pl.BlockSpec(memory_space=pltpu.SMEM)] + [pl.BlockSpec(memory_space=pl.ANY)] * 3,
        out_specs=pl.BlockSpec(memory_space=pl.ANY),
        scratch_shapes=[
            vmem((n, mb, nb), bf16),
            vmem((n, mb, mb), bf16),
            vmem((n, 2, 4, share, nb), bf16),
            vmem((pieces, LANES, nb), bf16),
            vmem((pieces, 2, 2, share, LANES), jnp.float32),
            vmem((pieces, 2, 2, share, LANES), bf16),
            vmem((pieces, 2, 2, share, LANES), bf16),
            vmem((pieces, 2, share, LANES), bf16),
            vmem((pieces, 2, share, LANES), bf16),
            vmem((pieces, share, LANES), bf16),
            vmem((pieces, share, LANES), bf16),
            vmem((pieces, share, LANES), bf16),
        ]
        + [dma((n,))] * 2
        + [dma((pieces,))] * 8
        + [dma((secs - 1, pieces))] * 2
        + [dma((pieces,))],
        compiler_params=pltpu.CompilerParams(
            collective_id=0, has_side_effects=True, vmem_limit_bytes=56 * 1024 * 1024
        ),
        cost_estimate=pl.CostEstimate(
            flops=2 * n * mb * nb * (mb + nb), bytes_accessed=20_000_000, transcendentals=0
        ),
    )(sec_rows, psi, normal_ops, comp_ops)
    return pl.pallas_call(
        place_kernel,
        out_shape=jax.ShapeDtypeStruct((n, share, nb), bf16),
        in_specs=[pl.BlockSpec(memory_space=pltpu.SMEM)] * 2
        + [pl.BlockSpec(memory_space=pltpu.VMEM)],
        out_specs=pl.BlockSpec(memory_space=pltpu.VMEM),
        scratch_shapes=[pltpu.SMEM((n,), jnp.int32)],
        compiler_params=pltpu.CompilerParams(vmem_limit_bytes=16 * 1024 * 1024),
    )(sec_rows, match, gathered)


def solution(mesh):
    in_specs = (
        P("sec", None, None),
        P(),
        P(),
        P("pair", "sec", None, None),
        P("pair", "sec", None, None),
    )
    out_specs = P("sec", "pair", None)
    body = shards
    if mesh.shape["pair"] == 8:
        body = functools.partial(kernel_shards, mesh.shape["sec"])
    return jax.shard_map(body, mesh=mesh, in_specs=in_specs, out_specs=out_specs, check_vma=False)
```
